512 devices in a mesh: band: 64 (over z, x_lo, core), fft: 8 (over x_hi, y).
Axes of the slice: x: 4 (x_hi: 2, x_lo: 2; x = x_hi * 2 + x_lo), y: 4, z: 16, core: 2. Of those that a mesh axis runs over, the one named last changes fastest.
Arguments:
- orbitals: float32 [128, 120, 14400], P('band', 'fft'), may hold values from -6 to 6
Outputs:
- exchange: float32 [128, 120, 14400], P('band', 'fft')
The draws below stay inside these ranges and needn't reach their ends.
All inputs are finite; a program needn't handle non-finite values.
Results may differ from the reference program's by a relative error of at most 0.0003.
Values sent between devices are 32-bit elements; how exact they have to be, the bound alone decides.
A program may use at most 64 MiB of HBM per device.

```python
import math
import jax
import jax.numpy as jnp
from jax import lax

NG = 120
ORB_DEV = 2
ORBITALS = 128
DIST = 16
N_BAND = 64


def draw_orbitals(key, part):
    key = jax.random.fold_in(key, 11)
    value_key = jax.random.fold_in(key, 1)
    values = jax.random.truncated_normal(value_key, -6.0, 6.0, (ORBITALS, NG, NG * NG), jnp.float32)
    return values.astype(jnp.float32)


def setup_inputs(seed: int = 0) -> dict:
    arg_keys = jax.random.split(jax.random.key(seed), 2)
    orbitals = draw_orbitals(jax.random.fold_in(arg_keys[1], 71), 0)
    return dict(orbitals=orbitals)


FRACTION = 0.25
CELL_BOHR = 37.25


def coulomb_kernel(size):
    index = jnp.arange(size, dtype=jnp.int32)
    whole = jnp.where(index <= size // 2, index, index - size).astype(jnp.float32)
    half = jnp.arange(size // 2 + 1, dtype=jnp.int32).astype(jnp.float32)
    step = 2.0 * math.pi / CELL_BOHR
    square = step ** 2 * (whole[:, None, None] ** 2 + whole[None, :, None] ** 2 + half[None, None, :] ** 2)
    safe = jnp.where(square > 0, square, jnp.float32(1.0))
    return jnp.where(square > 0, 4.0 * math.pi / safe, jnp.float32(0.0)).astype(jnp.float32)


def reference(orbitals):
    kernel = coulomb_kernel(NG)
    blocks = orbitals.reshape(N_BAND, ORB_DEV, NG, NG, NG)

    def one_field(codensity):
        spectrum = jnp.fft.rfftn(codensity)
        return jnp.fft.irfftn(spectrum * kernel, s=(NG, NG, NG)).astype(orbitals.dtype)

    def one_block(block_index):
        own = lax.dynamic_index_in_dim(blocks, block_index, 0, keepdims=False)
        partner = ((block_index - DIST) % N_BAND).astype(jnp.int32)
        visit = lax.dynamic_index_in_dim(blocks, partner, 0, keepdims=False)
        codensity = (own[:, None] * visit[None]).reshape(ORB_DEV * ORB_DEV, NG, NG, NG)
        fields = lax.map(one_field, codensity).reshape(ORB_DEV, ORB_DEV, NG, NG, NG)
        near = jnp.sum(fields * visit[None], axis=1)
        far = jnp.sum(fields * own[:, None], axis=0)
        return near, far

    near, far = lax.map(one_block, jnp.arange(N_BAND, dtype=jnp.int32))
    total = near + jnp.roll(far, -DIST, axis=0)
    return (-FRACTION * total).reshape(ORBITALS, NG, NG * NG)
```

```python
import functools
import math

import jax
import jax.numpy as jnp
import ml_dtypes
import numpy as np
from jax import lax
from jax.experimental import pallas as pl
from jax.experimental.pallas import tpu as pltpu
from jax.sharding import PartitionSpec as P

NG = 120
PLANES = 15
ROWS = 16
HALF = 64
GROUP = 8
COLS = HALF // GROUP
TILES = 113
PACKED = 1696
SPAN = PLANES * COLS
CHUNK = 5
FRACTION = 0.25
CELL_BOHR = 37.25
MESH = pl.DeviceIdType.MESH
f32, bf16 = jnp.float32, jnp.bfloat16


def split_const(table):
    high = table.astype(np.float32).astype(ml_dtypes.bfloat16)
    low = (table - high.astype(np.float64)).astype(np.float32).astype(ml_dtypes.bfloat16)
    return high, low


def on_left(table):
    high, low = split_const(table)
    return np.concatenate([high, high, low], axis=1)


def on_right(table):
    high, low = split_const(table)
    return np.concatenate([high, high, low], axis=0)


def tables():
    n = np.arange(NG)
    phase = (n[:, None] * n[None, :] % NG) * (2.0 * math.pi / NG)
    cos, sin = np.cos(phase), np.sin(phase)
    half = NG // 2 + 1
    first = np.zeros((2 * HALF, 128))
    first[:half, :NG] = cos[:half]
    first[HALF : HALF + half, :NG] = -sin[:half]
    wide_cos, wide_sin = np.zeros((128, 128)), np.zeros((128, 128))
    wide_cos[:NG, :NG], wide_sin[:NG, :NG] = cos, sin
    second = np.block([[wide_cos, -wide_sin], [wide_sin, wide_cos]])
    third = np.block([[cos, sin], [-sin, cos]])
    weight = np.full(half, 2.0)
    weight[[0, -1]] = 1.0
    weight *= -FRACTION / NG**3
    last = np.zeros((NG, 2 * HALF))
    last[:, :half] = cos[:, :half] * weight
    last[:, HALF : HALF + half] = -sin[:, :half] * weight
    return (
        on_left(first),
        on_right(second),
        on_left(third),
        on_left(third.T),
        on_right(second.T),
        on_left(last),
    )


def split(value):
    high = value.astype(bf16)
    return high, (value - high.astype(f32)).astype(bf16)


def left_dot(table, value):
    high, low = split(value)
    return jnp.dot(table, jnp.concatenate([high, low, high], axis=0), preferred_element_type=f32)


def right_dot(value, table):
    high, low = split(value)
    return jnp.dot(jnp.concatenate([high, low, high], axis=1), table, preferred_element_type=f32)


def kernel_body(
    steps,
    bands,
    x_ref,
    first_ref,
    second_ref,
    third_ref,
    third_back_ref,
    second_back_ref,
    last_ref,
    out_ref,
    own_in,
    vis_in,
    own,
    vis,
    near,
    far,
    scale,
    send_a,
    got_a,
    send_b,
    got_b,
    packed,
    back,
    in_send,
    in_recv,
    a_send,
    a_recv,
    b_send,
    b_recv,
    out_send,
    out_recv,
    keep_sem,
    go_sem,
):
    band = lax.axis_index("band")
    me = lax.axis_index("fft")
    core = lax.rem(band, 2)
    up = lax.rem(band + steps, bands)
    down = lax.rem(band + bands - steps, bands)
    mate = band + 1 - 2 * core

    barrier = pltpu.get_barrier_semaphore()
    for other in (up, down, mate):
        pl.semaphore_signal(barrier, 1, device_id=(other, me), device_id_type=MESH)
    for r in range(1, GROUP):
        pl.semaphore_signal(
            barrier, 1, device_id=(band, lax.rem(me + r, GROUP)), device_id_type=MESH
        )
    pl.semaphore_wait(barrier, GROUP + 2)

    def in_copy(kind, o):
        return pltpu.make_async_remote_copy(
            x_ref.at[:, o, :],
            (own_in, vis_in)[kind].at[o],
            in_send.at[kind, o],
            in_recv.at[kind, o],
            device_id=((down, up)[kind], me),
            device_id_type=MESH,
        )

    def out_copy(kind, o):
        return pltpu.make_async_remote_copy(
            packed.at[kind, o],
            back.at[kind, o],
            out_send.at[kind, o],
            out_recv.at[kind, o],
            device_id=((up, down)[kind], me),
            device_id_type=MESH,
        )

    def group_copy(sent, got, send_sem, recv_sem, pair, r):
        other = lax.rem(me + r, GROUP)
        return pltpu.make_async_remote_copy(
            sent.at[pair, :, pl.ds(pl.multiple_of(other * SPAN, 8), SPAN), :],
            got.at[pair, :, pl.ds(pl.multiple_of(me * SPAN, 8), SPAN), :],
            send_sem.at[pair, r],
            recv_sem.at[pair, r],
            device_id=(band, other),
            device_id_type=MESH,
        )

    def keep_copy(sent, got, stage, pair):
        place = pl.ds(pl.multiple_of(me * SPAN, 8), SPAN)
        return pltpu.make_async_copy(
            sent.at[pair, :, place, :], got.at[pair, :, place, :], keep_sem.at[stage, pair]
        )

    forth = (send_a, got_a, a_send, a_recv)
    return_trip = (send_b, got_b, b_send, b_recv)

    def start_group(stage, pair):
        arrays = (forth, return_trip)[stage]
        for r in range(1, GROUP):
            group_copy(*arrays, pair, r).start()
        keep_copy(arrays[0], arrays[1], stage, pair).start()

    def wait_group(stage, pair):
        arrays = (forth, return_trip)[stage]
        for r in range(1, GROUP):
            group_copy(*arrays, pair, r).wait_recv()
        keep_copy(arrays[0], arrays[1], stage, pair).wait()

    def wait_group_sent(stage, pair):
        arrays = (forth, return_trip)[stage]
        for r in range(1, GROUP):
            group_copy(*arrays, pair, r).wait_send()

    lane = lax.broadcasted_iota(jnp.int32, (PLANES, 128), 1)

    def unpack(source, target, o):
        def line(group, r, tile_start):
            if r == 0:
                return source[o, :, pl.ds(tile_start, 128)]
            before = source[o, :, pl.ds(tile_start - 128, 128)]
            if r == 16:
                return pltpu.roll(before, 128, 1)
            here = source[o, :, pl.ds(tile_start, 128)]
            return pltpu.roll(jnp.where(lane >= 128 - 8 * r, before, here), 8 * r, 1)

        def one_group(group, carry):
            for r in range(16):
                start = pl.multiple_of((group * 15 + r) * 128, 128)
                if r < 15:
                    value = line(group, r, start)
                else:
                    before = source[o, :, pl.ds(pl.multiple_of(start - 128, 128), 128)]
                    value = pltpu.roll(before, 120, 1)
                target[o, pl.ds(pl.multiple_of((group * 16 + r) * ROWS, 8), PLANES), :] = value
            return carry

        lax.fori_loop(0, 7, one_group, 0)
        for r in range(8):
            y = 112 + r
            if r < 7:
                value = line(7, r, (7 * 15 + r) * 128)
            else:
                value = jnp.concatenate(
                    [source[o, :, y * NG : (y + 1) * NG], jnp.zeros((PLANES, 8), f32)], axis=1
                )
            target[o, y * ROWS : y * ROWS + PLANES, :] = value

    def pack(source, kind, o):
        packed[kind, o, PACKED - 8 : PACKED, :] = jnp.zeros((8, 128), f32)

        def tile(y, s, following):
            value = source[o, pl.ds(pl.multiple_of(y * ROWS, 8), PLANES), :]
            if s:
                value = pltpu.roll(value, 128 - 8 * s, 1)
            if following is None:
                return value
            after = source[o, pl.ds(pl.multiple_of(following * ROWS, 8), PLANES), :]
            return jnp.where(lane < NG - 8 * s, value, pltpu.roll(after, NG - 8 * s, 1))

        def one_group(group, carry):
            for s in range(15):
                y = group * 16 + s
                packed[kind, o, pl.ds(group * 15 + s, PLANES, stride=TILES), :] = tile(y, s, y + 1)
            return carry

        lax.fori_loop(0, 7, one_group, 0)
        for s in range(8):
            y = 112 + s
            packed[kind, o, pl.ds(105 + s, PLANES, stride=TILES), :] = tile(
                y, s, y + 1 if s < 7 else None
            )

    def plane(ref, o, p):
        return ref[o, pl.ds(p, NG, stride=ROWS), :]

    def forward(pair):
        i, j = pair // 2, pair % 2

        def some_planes(step, carry):
            products = []
            for q in range(CHUNK):
                p = step * CHUNK + q
                product = plane(own, i, p) * plane(vis, j, p)
                products.append(jnp.concatenate([product, jnp.zeros((8, 128), f32)], axis=0))
            lines = left_dot(first_ref[...], jnp.concatenate(products, axis=1))
            lines = jnp.concatenate(
                [
                    jnp.concatenate(
                        [
                            lines[:HALF, q * 128 : (q + 1) * 128],
                            lines[HALF:, q * 128 : (q + 1) * 128],
                        ],
                        axis=1,
                    )
                    for q in range(CHUNK)
                ],
                axis=0,
            )
            spectrum = right_dot(lines, second_ref[...])
            for q in range(CHUNK):
                p = step * CHUNK + q
                for d in range(GROUP):
                    place = pl.ds(pl.multiple_of(d * SPAN + p * COLS, 8), COLS)
                    rows = slice(q * HALF + d * COLS, q * HALF + (d + 1) * COLS)
                    send_a[pair, 0, place, :] = spectrum[rows, :128]
                    send_a[pair, 1, place, :] = spectrum[rows, 128:]
            return carry

        lax.fori_loop(0, PLANES // CHUNK, some_planes, 0)

    def middle(pair):
        def two_columns(step, carry):
            columns = [step * 2, step * 2 + 1]
            data = jnp.concatenate(
                [
                    jnp.concatenate(
                        [
                            got_a[pair, 0, pl.ds(v, NG, stride=COLS), :],
                            got_a[pair, 1, pl.ds(v, NG, stride=COLS), :],
                        ],
                        axis=0,
                    )
                    for v in columns
                ],
                axis=1,
            )
            data = left_dot(third_ref[...], data)
            factor = jnp.concatenate([scale[v] for v in columns], axis=1)
            data = left_dot(
                third_back_ref[...], data * jnp.concatenate([factor, factor], axis=0)
            )
            for n, v in enumerate(columns):
                send_b[pair, 0, pl.ds(v, NG, stride=COLS), :] = data[
                    :NG, n * 128 : (n + 1) * 128
                ]
                send_b[pair, 1, pl.ds(v, NG, stride=COLS), :] = data[
                    NG:, n * 128 : (n + 1) * 128
                ]
            return carry

        lax.fori_loop(0, COLS // 2, two_columns, 0)

    def inverse(pair):
        i, j = pair // 2, pair % 2

        def some_planes(step, carry):
            spectra = []
            for q in range(CHUNK):
                p = step * CHUNK + q
                places = [pl.ds(pl.multiple_of(d * SPAN + p * COLS, 8), COLS) for d in range(GROUP)]
                spectra.append(
                    jnp.concatenate(
                        [
                            jnp.concatenate([got_b[pair, c, place, :] for place in places], axis=0)
                            for c in range(2)
                        ],
                        axis=1,
                    )
                )
            lines = right_dot(jnp.concatenate(spectra, axis=0), second_back_ref[...])
            lines = jnp.concatenate(
                [
                    jnp.concatenate(
                        [
                            lines[q * HALF : (q + 1) * HALF, :128],
                            lines[q * HALF : (q + 1) * HALF, 128:],
                        ],
                        axis=0,
                    )
                    for q in range(CHUNK)
                ],
                axis=1,
            )
            field = left_dot(last_ref[...], lines)
            for q in range(CHUNK):
                p = step * CHUNK + q
                value = field[:, q * 128 : (q + 1) * 128]
                to_near, to_far = plane(vis, j, p) * value, plane(own, i, p) * value
                if j:
                    to_near += plane(near, i, p)
                if i:
                    to_far += plane(far, j, p)
                near[i, pl.ds(p, NG, stride=ROWS), :] = to_near
                far[j, pl.ds(p, NG, stride=ROWS), :] = to_far
            return carry

        lax.fori_loop(0, PLANES // CHUNK, some_planes, 0)

    def fold(index):
        return jnp.where(index <= NG // 2, index, index - NG).astype(f32)

    def prepare_scale():
        step = 2.0 * math.pi / CELL_BOHR
        second = fold(lax.broadcasted_iota(jnp.int32, (NG, 128), 0))
        third = fold(lax.broadcasted_iota(jnp.int32, (NG, 128), 1))
        flat = second * second + third * third

        def column(v, carry):
            first = (me * COLS + v).astype(f32)
            square = step**2 * (flat + first * first)
            safe = jnp.where(square > 0, square, 1.0)
            scale[v] = jnp.where(square > 0, 4.0 * math.pi / safe, 0.0)
            return carry

        lax.fori_loop(0, COLS, column, 0)

    def finish(o):
        def one_tile(t, carry):
            rows = pl.ds(t, PLANES, stride=TILES)
            out_ref[o, :, pl.ds(pl.multiple_of(t * 128, 128), 128)] = (
                back[0, o, rows, :] + back[1, o, rows, :]
            )
            return carry

        lax.fori_loop(0, TILES - 1, one_tile, 0)
        rows = pl.ds(TILES - 1, PLANES, stride=TILES)
        total = back[0, o, rows, :] + back[1, o, rows, :]
        out_ref[o, :, (TILES - 1) * 128 :] = total[:, : NG * NG - (TILES - 1) * 128]

    @pl.when(core == 1)
    def _():
        pl.semaphore_wait(go_sem, 1)

    for o in range(2):
        for kind in range(2):
            in_copy(kind, o).start()
    prepare_scale()

    for kind in range(2):
        in_copy(kind, 0).wait_recv()
    unpack(own_in, own, 0)
    unpack(vis_in, vis, 0)
    forward(0)
    start_group(0, 0)

    for o in range(2):
        for kind in range(2):
            in_copy(kind, o).wait_send()

    @pl.when(core == 0)
    def _():
        pl.semaphore_signal(go_sem, 1, device_id=(mate, me), device_id_type=MESH)

    for kind in range(2):
        in_copy(kind, 1).wait_recv()
    unpack(vis_in, vis, 1)
    forward(1)
    start_group(0, 1)
    wait_group(0, 0)
    middle(0)
    start_group(1, 0)
    unpack(own_in, own, 1)
    forward(2)
    start_group(0, 2)
    wait_group(0, 1)
    middle(1)
    start_group(1, 1)
    wait_group(1, 0)
    inverse(0)
    forward(3)
    start_group(0, 3)
    wait_group(0, 2)
    middle(2)
    start_group(1, 2)
    wait_group(1, 1)
    inverse(1)
    pack(near, 0, 0)
    out_copy(0, 0).start()
    wait_group(0, 3)
    middle(3)
    start_group(1, 3)
    wait_group(1, 2)
    inverse(2)
    pack(far, 1, 0)
    out_copy(1, 0).start()
    wait_group(1, 3)
    inverse(3)
    pack(near, 0, 1)
    out_copy(0, 1).start()
    pack(far, 1, 1)
    out_copy(1, 1).start()

    for stage in range(2):
        for pair in range(4):
            wait_group_sent(stage, pair)
    for o in range(2):
        for kind in range(2):
            out_copy(kind, o).wait_recv()
        finish(o)
    for o in range(2):
        for kind in range(2):
            out_copy(kind, o).wait_send()


def body(orbitals):
    bands = lax.axis_size("band")
    steps = bands // 8
    whole = pl.BlockSpec(memory_space=pltpu.VMEM)
    lines = NG * ROWS
    dma = pltpu.SemaphoreType.DMA
    return pl.pallas_call(
        functools.partial(kernel_body, steps, bands),
        out_shape=jax.ShapeDtypeStruct(orbitals.shape, f32),
        in_specs=[pl.BlockSpec(memory_space=pl.ANY)] + [whole] * 6,
        out_specs=whole,
        scratch_shapes=[
            pltpu.VMEM((2, PLANES, NG * NG), f32),
            pltpu.VMEM((2, PLANES, NG * NG), f32),
            pltpu.VMEM((2, lines, 128), f32),
            pltpu.VMEM((2, lines, 128), f32),
            pltpu.VMEM((2, lines, 128), f32),
            pltpu.VMEM((2, lines, 128), f32),
            pltpu.VMEM((COLS, NG, 128), f32),
            pltpu.VMEM((4, 2, GROUP * SPAN, 128), f32),
            pltpu.VMEM((4, 2, GROUP * SPAN, 128), f32),
            pltpu.VMEM((4, 2, GROUP * SPAN, 128), f32),
            pltpu.VMEM((4, 2, GROUP * SPAN, 128), f32),
            pltpu.VMEM((2, 2, PACKED, 128), f32),
            pltpu.VMEM((2, 2, PACKED, 128), f32),
            dma((2, 2)),
            dma((2, 2)),
            dma((4, GROUP)),
            dma((4, GROUP)),
            dma((4, GROUP)),
            dma((4, GROUP)),
            dma((2, 2)),
            dma((2, 2)),
            dma((2, 4)),
            pltpu.SemaphoreType.REGULAR,
        ],
        compiler_params=pltpu.CompilerParams(
            collective_id=0, has_side_effects=True, vmem_limit_bytes=56 << 20
        ),
    )(orbitals.transpose(1, 0, 2), *(jnp.asarray(t) for t in tables()))


def solution(mesh):
    return jax.shard_map(
        body,
        mesh=mesh,
        in_specs=(P("band", "fft", None),),
        out_specs=P("band", "fft", None),
        check_vma=False,
    )
```

```python
import functools
import math

import jax
import jax.numpy as jnp
import ml_dtypes
import numpy as np
from jax import lax
from jax.experimental import pallas as pl
from jax.experimental.pallas import tpu as pltpu
from jax.sharding import PartitionSpec as P

NG = 120
PLANES = 15
HALF = 64
GROUP = 8
COLS = HALF // GROUP
SPAN = PLANES * COLS
CHUNK = 5
FRACTION = 0.25
CELL_BOHR = 37.25
MESH = pl.DeviceIdType.MESH
f32, bf16 = jnp.float32, jnp.bfloat16


def split_const(table):
    high = table.astype(np.float32).astype(ml_dtypes.bfloat16)
    low = (table - high.astype(np.float64)).astype(np.float32).astype(ml_dtypes.bfloat16)
    return high, low


def on_left(table):
    high, low = split_const(table)
    return np.concatenate([high, high, low], axis=1)


def on_right(table):
    high, low = split_const(table)
    return np.concatenate([high, high, low], axis=0)


def tables():
    n = np.arange(NG)
    phase = (n[:, None] * n[None, :] % NG) * (2.0 * math.pi / NG)
    cos, sin = np.cos(phase), np.sin(phase)
    half = NG // 2 + 1
    first = np.zeros((2 * HALF, 128))
    first[:half, :NG] = cos[:half]
    first[HALF : HALF + half, :NG] = -sin[:half]
    wide_cos, wide_sin = np.zeros((128, 128)), np.zeros((128, 128))
    wide_cos[:NG, :NG], wide_sin[:NG, :NG] = cos, sin
    second = np.block([[wide_cos, -wide_sin], [wide_sin, wide_cos]])
    third = np.block([[cos, sin], [-sin, cos]])
    weight = np.full(half, 2.0)
    weight[[0, -1]] = 1.0
    weight *= -FRACTION / NG**3
    last = np.zeros((NG, 2 * HALF))
    last[:, :half] = cos[:, :half] * weight
    last[:, HALF : HALF + half] = -sin[:, :half] * weight
    return (
        on_left(first),
        on_right(second),
        on_left(third),
        on_left(third.T),
        on_right(second.T),
        on_left(last),
    )


def split(value):
    high = value.astype(bf16)
    return high, (value - high.astype(f32)).astype(bf16)


def left_dot(table, value):
    high, low = split(value)
    return jnp.dot(table, jnp.concatenate([high, low, high], axis=0), preferred_element_type=f32)


def right_dot(value, table):
    high, low = split(value)
    return jnp.dot(jnp.concatenate([high, low, high], axis=1), table, preferred_element_type=f32)


def kernel_body(
    steps,
    bands,
    x_ref,
    first_ref,
    second_ref,
    third_ref,
    third_back_ref,
    second_back_ref,
    last_ref,
    near_ref,
    far_ref,
    own_in,
    vis_in,
    own,
    vis,
    near,
    far,
    scale,
    send_a,
    got_a,
    send_b,
    got_b,
    packed,
    in_send,
    in_recv,
    a_send,
    a_recv,
    b_send,
    b_recv,
    out_send,
    out_recv,
    keep_sem,
    go_sem,
):
    band = lax.axis_index("band")
    me = lax.axis_index("fft")
    core = lax.rem(band, 2)
    up = lax.rem(band + steps, bands)
    down = lax.rem(band + bands - steps, bands)
    mate = band + 1 - 2 * core

    barrier = pltpu.get_barrier_semaphore()
    for other in (up, down, mate):
        pl.semaphore_signal(barrier, 1, device_id=(other, me), device_id_type=MESH)
    for r in range(1, GROUP):
        pl.semaphore_signal(
            barrier, 1, device_id=(band, lax.rem(me + r, GROUP)), device_id_type=MESH
        )
    pl.semaphore_wait(barrier, GROUP + 2)

    def in_copy(kind, o):
        return pltpu.make_async_remote_copy(
            x_ref.at[:, o, :],
            (own_in, vis_in)[kind].at[o],
            in_send.at[kind, o],
            in_recv.at[kind, o],
            device_id=((down, up)[kind], me),
            device_id_type=MESH,
        )

    def out_copy(kind, o):
        return pltpu.make_async_remote_copy(
            packed.at[kind, o],
            (near_ref, far_ref)[kind].at[:, o, :],
            out_send.at[kind, o],
            out_recv.at[kind, o],
            device_id=((up, down)[kind], me),
            device_id_type=MESH,
        )

    def group_copy(sent, got, send_sem, recv_sem, pair, r):
        other = lax.rem(me + r, GROUP)
        return pltpu.make_async_remote_copy(
            sent.at[pair, :, pl.ds(pl.multiple_of(other * SPAN, 8), SPAN), :],
            got.at[pair, :, pl.ds(pl.multiple_of(me * SPAN, 8), SPAN), :],
            send_sem.at[pair, r],
            recv_sem.at[pair, r],
            device_id=(band, other),
            device_id_type=MESH,
        )

    def keep_copy(sent, got, stage, pair):
        place = pl.ds(pl.multiple_of(me * SPAN, 8), SPAN)
        return pltpu.make_async_copy(
            sent.at[pair, :, place, :], got.at[pair, :, place, :], keep_sem.at[stage, pair]
        )

    forth = (send_a, got_a, a_send, a_recv)
    return_trip = (send_b, got_b, b_send, b_recv)

    def start_group(stage, pair):
        arrays = (forth, return_trip)[stage]
        for r in range(1, GROUP):
            group_copy(*arrays, pair, r).start()
        keep_copy(arrays[0], arrays[1], stage, pair).start()

    def wait_group(stage, pair):
        arrays = (forth, return_trip)[stage]
        for r in range(1, GROUP):
            group_copy(*arrays, pair, r).wait_recv()
        keep_copy(arrays[0], arrays[1], stage, pair).wait()

    def wait_group_sent(stage, pair):
        arrays = (forth, return_trip)[stage]
        for r in range(1, GROUP):
            group_copy(*arrays, pair, r).wait_send()

    lane = lax.broadcasted_iota(jnp.int32, (PLANES, 128), 1)

    def unpack(source, target, o):
        def line(group, r, tile_start):
            if r == 0:
                return source[o, :, pl.ds(tile_start, 128)]
            before = source[o, :, pl.ds(tile_start - 128, 128)]
            if r == 16:
                return pltpu.roll(before, 128, 1)
            here = source[o, :, pl.ds(tile_start, 128)]
            return pltpu.roll(jnp.where(lane >= 128 - 8 * r, before, here), 8 * r, 1)

        def one_group(group, carry):
            for r in range(16):
                start = pl.multiple_of((group * 15 + r) * 128, 128)
                if r < 15:
                    value = line(group, r, start)
                else:
                    before = source[o, :, pl.ds(pl.multiple_of(start - 128, 128), 128)]
                    value = pltpu.roll(before, 120, 1)
                target[o, pl.ds(group * 16 + r, PLANES, stride=NG), :] = value
            return carry

        lax.fori_loop(0, 7, one_group, 0)
        for r in range(8):
            y = 112 + r
            if r < 7:
                value = line(7, r, (7 * 15 + r) * 128)
            else:
                value = jnp.concatenate(
                    [source[o, :, y * NG : (y + 1) * NG], jnp.zeros((PLANES, 8), f32)], axis=1
                )
            target[o, pl.ds(y, PLANES, stride=NG), :] = value

    def pack(source, kind, o):
        def tile(y, s, following):
            value = source[o, pl.ds(y, PLANES, stride=NG), :]
            if s:
                value = pltpu.roll(value, 128 - 8 * s, 1)
            if following is None:
                return value
            after = source[o, pl.ds(following, PLANES, stride=NG), :]
            return jnp.where(lane < NG - 8 * s, value, pltpu.roll(after, NG - 8 * s, 1))

        def one_group(group, carry):
            for s in range(15):
                y = group * 16 + s
                place = pl.ds(pl.multiple_of((group * 15 + s) * 128, 128), 128)
                packed[kind, o, :, place] = tile(y, s, y + 1)
            return carry

        lax.fori_loop(0, 7, one_group, 0)
        for s in range(8):
            y = 112 + s
            start = (105 + s) * 128
            if s < 7:
                packed[kind, o, :, start : start + 128] = tile(y, s, y + 1)
            else:
                packed[kind, o, :, start:] = tile(y, s, None)[:, : NG * NG - start]

    def plane(ref, o, p):
        return ref[o, pl.ds(pl.multiple_of(p * NG, 8), NG), :]

    def forward(pair):
        i, j = pair // 2, pair % 2

        def some_planes(step, carry):
            products = []
            for q in range(CHUNK):
                p = step * CHUNK + q
                product = plane(own, i, p) * plane(vis, j, p)
                products.append(jnp.concatenate([product, jnp.zeros((8, 128), f32)], axis=0))
            lines = left_dot(first_ref[...], jnp.concatenate(products, axis=1))
            lines = jnp.concatenate(
                [
                    jnp.concatenate(
                        [
                            lines[:HALF, q * 128 : (q + 1) * 128],
                            lines[HALF:, q * 128 : (q + 1) * 128],
                        ],
                        axis=1,
                    )
                    for q in range(CHUNK)
                ],
                axis=0,
            )
            spectrum = right_dot(lines, second_ref[...])
            for q in range(CHUNK):
                p = step * CHUNK + q
                for d in range(GROUP):
                    place = pl.ds(pl.multiple_of(d * SPAN + p * COLS, 8), COLS)
                    rows = slice(q * HALF + d * COLS, q * HALF + (d + 1) * COLS)
                    send_a[pair, 0, place, :] = spectrum[rows, :128]
                    send_a[pair, 1, place, :] = spectrum[rows, 128:]
            return carry

        lax.fori_loop(0, PLANES // CHUNK, some_planes, 0)

    def middle(pair):
        def two_columns(step, carry):
            columns = [step * 2, step * 2 + 1]
            data = jnp.concatenate(
                [
                    jnp.concatenate(
                        [
                            got_a[pair, 0, pl.ds(v, NG, stride=COLS), :],
                            got_a[pair, 1, pl.ds(v, NG, stride=COLS), :],
                        ],
                        axis=0,
                    )
                    for v in columns
                ],
                axis=1,
            )
            data = left_dot(third_ref[...], data)
            factor = jnp.concatenate([scale[v] for v in columns], axis=1)
            data = left_dot(
                third_back_ref[...], data * jnp.concatenate([factor, factor], axis=0)
            )
            for n, v in enumerate(columns):
                send_b[pair, 0, pl.ds(v, NG, stride=COLS), :] = data[
                    :NG, n * 128 : (n + 1) * 128
                ]
                send_b[pair, 1, pl.ds(v, NG, stride=COLS), :] = data[
                    NG:, n * 128 : (n + 1) * 128
                ]
            return carry

        lax.fori_loop(0, COLS // 2, two_columns, 0)

    def inverse(pair):
        i, j = pair // 2, pair % 2

        def some_planes(step, carry):
            spectra = []
            for q in range(CHUNK):
                p = step * CHUNK + q
                places = [pl.ds(pl.multiple_of(d * SPAN + p * COLS, 8), COLS) for d in range(GROUP)]
                spectra.append(
                    jnp.concatenate(
                        [
                            jnp.concatenate([got_b[pair, c, place, :] for place in places], axis=0)
                            for c in range(2)
                        ],
                        axis=1,
                    )
                )
            lines = right_dot(jnp.concatenate(spectra, axis=0), second_back_ref[...])
            lines = jnp.concatenate(
                [
                    jnp.concatenate(
                        [
                            lines[q * HALF : (q + 1) * HALF, :128],
                            lines[q * HALF : (q + 1) * HALF, 128:],
                        ],
                        axis=0,
                    )
                    for q in range(CHUNK)
                ],
                axis=1,
            )
            field = left_dot(last_ref[...], lines)
            for q in range(CHUNK):
                p = step * CHUNK + q
                value = field[:, q * 128 : (q + 1) * 128]
                to_near, to_far = plane(vis, j, p) * value, plane(own, i, p) * value
                if j:
                    to_near += plane(near, i, p)
                if i:
                    to_far += plane(far, j, p)
                near[i, pl.ds(pl.multiple_of(p * NG, 8), NG), :] = to_near
                far[j, pl.ds(pl.multiple_of(p * NG, 8), NG), :] = to_far
            return carry

        lax.fori_loop(0, PLANES // CHUNK, some_planes, 0)

    def fold(index):
        return jnp.where(index <= NG // 2, index, index - NG).astype(f32)

    def prepare_scale():
        step = 2.0 * math.pi / CELL_BOHR
        second = fold(lax.broadcasted_iota(jnp.int32, (NG, 128), 0))
        third = fold(lax.broadcasted_iota(jnp.int32, (NG, 128), 1))
        flat = second * second + third * third

        def column(v, carry):
            first = (me * COLS + v).astype(f32)
            square = step**2 * (flat + first * first)
            safe = jnp.where(square > 0, square, 1.0)
            scale[v] = jnp.where(square > 0, 4.0 * math.pi / safe, 0.0)
            return carry

        lax.fori_loop(0, COLS, column, 0)

    @pl.when(core == 1)
    def _():
        pl.semaphore_wait(go_sem, 1)

    for o in range(2):
        for kind in range(2):
            in_copy(kind, o).start()
    prepare_scale()

    for kind in range(2):
        in_copy(kind, 0).wait_recv()
    unpack(own_in, own, 0)
    unpack(vis_in, vis, 0)
    forward(0)
    start_group(0, 0)
    wait_group(0, 0)
    middle(0)
    start_group(1, 0)

    for o in range(2):
        for kind in range(2):
            in_copy(kind, o).wait_send()

    @pl.when(core == 0)
    def _():
        pl.semaphore_signal(go_sem, 1, device_id=(mate, me), device_id_type=MESH)

    in_copy(1, 1).wait_recv()
    unpack(vis_in, vis, 1)
    forward(1)
    start_group(0, 1)
    in_copy(0, 1).wait_recv()
    unpack(own_in, own, 1)
    forward(2)
    start_group(0, 2)
    forward(3)
    start_group(0, 3)
    wait_group(1, 0)
    inverse(0)
    for pair in range(1, 4):
        wait_group(0, pair)
        middle(pair)
        start_group(1, pair)
    wait_group(1, 1)
    inverse(1)
    pack(near, 0, 0)
    out_copy(0, 0).start()
    wait_group(1, 2)
    inverse(2)
    pack(far, 1, 0)
    out_copy(1, 0).start()
    wait_group(1, 3)
    inverse(3)
    pack(near, 0, 1)
    out_copy(0, 1).start()
    pack(far, 1, 1)
    out_copy(1, 1).start()

    for stage in range(2):
        for pair in range(4):
            wait_group_sent(stage, pair)
    for o in range(2):
        for kind in range(2):
            out_copy(kind, o).wait_recv()
    for o in range(2):
        for kind in range(2):
            out_copy(kind, o).wait_send()


def body(orbitals):
    bands = lax.axis_size("band")
    steps = bands // 8
    whole = pl.BlockSpec(memory_space=pltpu.VMEM)
    lines = NG * PLANES
    dma = pltpu.SemaphoreType.DMA
    by_plane = orbitals.transpose(1, 0, 2)
    sums = jax.ShapeDtypeStruct(by_plane.shape, f32)
    near, far = pl.pallas_call(
        functools.partial(kernel_body, steps, bands),
        out_shape=(sums, sums),
        in_specs=[pl.BlockSpec(memory_space=pl.ANY)] + [whole] * 6,
        out_specs=(pl.BlockSpec(memory_space=pl.ANY), pl.BlockSpec(memory_space=pl.ANY)),
        scratch_shapes=[
            pltpu.VMEM((2, PLANES, NG * NG), f32),
            pltpu.VMEM((2, PLANES, NG * NG), f32),
            pltpu.VMEM((2, lines, 128), f32),
            pltpu.VMEM((2, lines, 128), f32),
            pltpu.VMEM((2, lines, 128), f32),
            pltpu.VMEM((2, lines, 128), f32),
            pltpu.VMEM((COLS, NG, 128), f32),
            pltpu.VMEM((4, 2, GROUP * SPAN, 128), f32),
            pltpu.VMEM((4, 2, GROUP * SPAN, 128), f32),
            pltpu.VMEM((4, 2, GROUP * SPAN, 128), f32),
            pltpu.VMEM((4, 2, GROUP * SPAN, 128), f32),
            pltpu.VMEM((2, 2, PLANES, NG * NG), f32),
            dma((2, 2)),
            dma((2, 2)),
            dma((4, GROUP)),
            dma((4, GROUP)),
            dma((4, GROUP)),
            dma((4, GROUP)),
            dma((2, 2)),
            dma((2, 2)),
            dma((2, 4)),
            pltpu.SemaphoreType.REGULAR,
        ],
        compiler_params=pltpu.CompilerParams(
            collective_id=0, has_side_effects=True, vmem_limit_bytes=56 << 20
        ),
    )(by_plane, *(jnp.asarray(t) for t in tables()))
    return (near + far).transpose(1, 0, 2)


def solution(mesh):
    return jax.shard_map(
        body,
        mesh=mesh,
        in_specs=(P("band", "fft", None),),
        out_specs=P("band", "fft", None),
        check_vma=False,
    )
```

```python
import functools
import math

import jax
import jax.numpy as jnp
import ml_dtypes
import numpy as np
from jax import lax
from jax.experimental import pallas as pl
from jax.experimental.pallas import tpu as pltpu
from jax.sharding import PartitionSpec as P

NG = 120
PLANES = 15
HALF = 64
GROUP = 8
COLS = HALF // GROUP
SPAN = PLANES * COLS
CHUNK = 5
FRACTION = 0.25
CELL_BOHR = 37.25
MESH = pl.DeviceIdType.MESH
f32, bf16 = jnp.float32, jnp.bfloat16


def split_const(table):
    high = table.astype(np.float32).astype(ml_dtypes.bfloat16)
    low = (table - high.astype(np.float64)).astype(np.float32).astype(ml_dtypes.bfloat16)
    return high, low


def on_left(table):
    high, low = split_const(table)
    return np.concatenate([high, high, low], axis=1)


def on_right(table):
    high, low = split_const(table)
    return np.concatenate([high, high, low], axis=0)


def tables():
    n = np.arange(NG)
    phase = (n[:, None] * n[None, :] % NG) * (2.0 * math.pi / NG)
    cos, sin = np.cos(phase), np.sin(phase)
    half = NG // 2 + 1
    first = np.zeros((2 * HALF, 128))
    first[:half, :NG] = cos[:half]
    first[HALF : HALF + half, :NG] = -sin[:half]
    wide_cos, wide_sin = np.zeros((128, 128)), np.zeros((128, 128))
    wide_cos[:NG, :NG], wide_sin[:NG, :NG] = cos, sin
    second = np.block([[wide_cos, -wide_sin], [wide_sin, wide_cos]])
    third = np.block([[cos, sin], [-sin, cos]])
    weight = np.full(half, 2.0)
    weight[[0, -1]] = 1.0
    weight *= -FRACTION / NG**3
    last = np.zeros((NG, 2 * HALF))
    last[:, :half] = cos[:, :half] * weight
    last[:, HALF : HALF + half] = -sin[:, :half] * weight
    return (
        on_left(first),
        on_right(second),
        on_left(third),
        on_left(third.T),
        on_right(second.T),
        on_left(last),
    )


def split(value):
    high = value.astype(bf16)
    return high, (value - high.astype(f32)).astype(bf16)


def left_dot(table, value):
    high, low = split(value)
    return jnp.dot(table, jnp.concatenate([high, low, high], axis=0), preferred_element_type=f32)


def right_dot(value, table):
    high, low = split(value)
    return jnp.dot(jnp.concatenate([high, low, high], axis=1), table, preferred_element_type=f32)


def kernel_body(
    steps,
    bands,
    x_ref,
    first_ref,
    second_ref,
    third_ref,
    third_back_ref,
    second_back_ref,
    last_ref,
    near_ref,
    far_ref,
    own_in,
    vis_in,
    own,
    vis,
    near,
    far,
    scale,
    send_a,
    got_a,
    send_b,
    got_b,
    packed,
    in_send,
    in_recv,
    a_send,
    a_recv,
    b_send,
    b_recv,
    out_send,
    out_recv,
    keep_sem,
    go_sem,
):
    band = lax.axis_index("band")
    me = lax.axis_index("fft")
    core = lax.rem(band, 2)
    up = lax.rem(band + steps, bands)
    down = lax.rem(band + bands - steps, bands)
    mate = band + 1 - 2 * core
    chip = bands // 16
    odd = lax.rem(lax.div(band, chip), 2)
    beside = [
        lax.rem(first + step + bands, bands) for first in (band, mate) for step in (chip, -chip)
    ]

    barrier = pltpu.get_barrier_semaphore()
    for other in (up, down, *beside):
        pl.semaphore_signal(barrier, 1, device_id=(other, me), device_id_type=MESH)
    for r in range(1, GROUP):
        pl.semaphore_signal(
            barrier, 1, device_id=(band, lax.rem(me + r, GROUP)), device_id_type=MESH
        )
    pl.semaphore_wait(barrier, GROUP + 5)

    def in_copy(kind, o, part):
        place = pl.ds(*((0, 11264), (11264, 3136))[part])
        return pltpu.make_async_remote_copy(
            x_ref.at[:, o, place],
            (own_in, vis_in)[kind].at[o, :, place],
            in_send.at[kind, o, part],
            in_recv.at[kind, o, part],
            device_id=((down, up)[kind], me),
            device_id_type=MESH,
        )

    def out_copy(kind, o):
        return pltpu.make_async_remote_copy(
            packed.at[kind, o],
            (near_ref, far_ref)[kind].at[:, o, :],
            out_send.at[kind, o],
            out_recv.at[kind, o],
            device_id=((up, down)[kind], me),
            device_id_type=MESH,
        )

    def group_copy(sent, got, send_sem, recv_sem, pair, r):
        other = lax.rem(me + r, GROUP)
        return pltpu.make_async_remote_copy(
            sent.at[pair, :, pl.ds(pl.multiple_of(other * SPAN, 8), SPAN), :],
            got.at[pair, :, pl.ds(pl.multiple_of(me * SPAN, 8), SPAN), :],
            send_sem.at[pair, r],
            recv_sem.at[pair, r],
            device_id=(band, other),
            device_id_type=MESH,
        )

    def keep_copy(sent, got, stage, pair):
        place = pl.ds(pl.multiple_of(me * SPAN, 8), SPAN)
        return pltpu.make_async_copy(
            sent.at[pair, :, place, :], got.at[pair, :, place, :], keep_sem.at[stage, pair]
        )

    forth = (send_a, got_a, a_send, a_recv)
    return_trip = (send_b, got_b, b_send, b_recv)

    def start_group(stage, pair):
        arrays = (forth, return_trip)[stage]
        for r in range(1, GROUP):
            group_copy(*arrays, pair, r).start()
        keep_copy(arrays[0], arrays[1], stage, pair).start()

    def wait_group(stage, pair):
        arrays = (forth, return_trip)[stage]
        for r in range(1, GROUP):
            group_copy(*arrays, pair, r).wait_recv()
        keep_copy(arrays[0], arrays[1], stage, pair).wait()

    def wait_group_sent(stage, pair):
        arrays = (forth, return_trip)[stage]
        for r in range(1, GROUP):
            group_copy(*arrays, pair, r).wait_send()

    lane = lax.broadcasted_iota(jnp.int32, (PLANES, 128), 1)

    def unpack(source, target, o):
        def line(group, r, tile_start):
            if r == 0:
                return source[o, :, pl.ds(tile_start, 128)]
            before = source[o, :, pl.ds(tile_start - 128, 128)]
            if r == 16:
                return pltpu.roll(before, 128, 1)
            here = source[o, :, pl.ds(tile_start, 128)]
            return pltpu.roll(jnp.where(lane >= 128 - 8 * r, before, here), 8 * r, 1)

        def one_group(group, carry):
            for r in range(16):
                start = pl.multiple_of((group * 15 + r) * 128, 128)
                if r < 15:
                    value = line(group, r, start)
                else:
                    before = source[o, :, pl.ds(pl.multiple_of(start - 128, 128), 128)]
                    value = pltpu.roll(before, 120, 1)
                target[o, pl.ds(group * 16 + r, PLANES, stride=NG), :] = value
            return carry

        lax.fori_loop(0, 7, one_group, 0)
        for r in range(8):
            y = 112 + r
            if r < 7:
                value = line(7, r, (7 * 15 + r) * 128)
            else:
                value = jnp.concatenate(
                    [source[o, :, y * NG : (y + 1) * NG], jnp.zeros((PLANES, 8), f32)], axis=1
                )
            target[o, pl.ds(y, PLANES, stride=NG), :] = value

    def pack(source, kind, o):
        def tile(y, s, following):
            value = source[o, pl.ds(y, PLANES, stride=NG), :]
            if s:
                value = pltpu.roll(value, 128 - 8 * s, 1)
            if following is None:
                return value
            after = source[o, pl.ds(following, PLANES, stride=NG), :]
            return jnp.where(lane < NG - 8 * s, value, pltpu.roll(after, NG - 8 * s, 1))

        def one_group(group, carry):
            for s in range(15):
                y = group * 16 + s
                place = pl.ds(pl.multiple_of((group * 15 + s) * 128, 128), 128)
                packed[kind, o, :, place] = tile(y, s, y + 1)
            return carry

        lax.fori_loop(0, 7, one_group, 0)
        for s in range(8):
            y = 112 + s
            start = (105 + s) * 128
            if s < 7:
                packed[kind, o, :, start : start + 128] = tile(y, s, y + 1)
            else:
                packed[kind, o, :, start:] = tile(y, s, None)[:, : NG * NG - start]

    def plane(ref, o, p):
        return ref[o, pl.ds(pl.multiple_of(p * NG, 8), NG), :]

    def forward(pair):
        i, j = pair // 2, pair % 2

        def some_planes(step, carry):
            products = []
            for q in range(CHUNK):
                p = step * CHUNK + q
                product = plane(own, i, p) * plane(vis, j, p)
                products.append(jnp.concatenate([product, jnp.zeros((8, 128), f32)], axis=0))
            lines = left_dot(first_ref[...], jnp.concatenate(products, axis=1))
            lines = jnp.concatenate(
                [
                    jnp.concatenate(
                        [
                            lines[:HALF, q * 128 : (q + 1) * 128],
                            lines[HALF:, q * 128 : (q + 1) * 128],
                        ],
                        axis=1,
                    )
                    for q in range(CHUNK)
                ],
                axis=0,
            )
            spectrum = right_dot(lines, second_ref[...])
            for q in range(CHUNK):
                p = step * CHUNK + q
                for d in range(GROUP):
                    place = pl.ds(pl.multiple_of(d * SPAN + p * COLS, 8), COLS)
                    rows = slice(q * HALF + d * COLS, q * HALF + (d + 1) * COLS)
                    send_a[pair, 0, place, :] = spectrum[rows, :128]
                    send_a[pair, 1, place, :] = spectrum[rows, 128:]
            return carry

        lax.fori_loop(0, PLANES // CHUNK, some_planes, 0)

    def middle(pair):
        def two_columns(step, carry):
            columns = [step * 2, step * 2 + 1]
            data = jnp.concatenate(
                [
                    jnp.concatenate(
                        [
                            got_a[pair, 0, pl.ds(v, NG, stride=COLS), :],
                            got_a[pair, 1, pl.ds(v, NG, stride=COLS), :],
                        ],
                        axis=0,
                    )
                    for v in columns
                ],
                axis=1,
            )
            data = left_dot(third_ref[...], data)
            factor = jnp.concatenate([scale[v] for v in columns], axis=1)
            data = left_dot(
                third_back_ref[...], data * jnp.concatenate([factor, factor], axis=0)
            )
            for n, v in enumerate(columns):
                send_b[pair, 0, pl.ds(v, NG, stride=COLS), :] = data[
                    :NG, n * 128 : (n + 1) * 128
                ]
                send_b[pair, 1, pl.ds(v, NG, stride=COLS), :] = data[
                    NG:, n * 128 : (n + 1) * 128
                ]
            return carry

        lax.fori_loop(0, COLS // 2, two_columns, 0)

    def inverse(pair):
        i, j = pair // 2, pair % 2

        def some_planes(step, carry):
            spectra = []
            for q in range(CHUNK):
                p = step * CHUNK + q
                places = [pl.ds(pl.multiple_of(d * SPAN + p * COLS, 8), COLS) for d in range(GROUP)]
                spectra.append(
                    jnp.concatenate(
                        [
                            jnp.concatenate([got_b[pair, c, place, :] for place in places], axis=0)
                            for c in range(2)
                        ],
                        axis=1,
                    )
                )
            lines = right_dot(jnp.concatenate(spectra, axis=0), second_back_ref[...])
            lines = jnp.concatenate(
                [
                    jnp.concatenate(
                        [
                            lines[q * HALF : (q + 1) * HALF, :128],
                            lines[q * HALF : (q + 1) * HALF, 128:],
                        ],
                        axis=0,
                    )
                    for q in range(CHUNK)
                ],
                axis=1,
            )
            field = left_dot(last_ref[...], lines)
            for q in range(CHUNK):
                p = step * CHUNK + q
                value = field[:, q * 128 : (q + 1) * 128]
                to_near, to_far = plane(vis, j, p) * value, plane(own, i, p) * value
                if j:
                    to_near += plane(near, i, p)
                if i:
                    to_far += plane(far, j, p)
                near[i, pl.ds(pl.multiple_of(p * NG, 8), NG), :] = to_near
                far[j, pl.ds(pl.multiple_of(p * NG, 8), NG), :] = to_far
            return carry

        lax.fori_loop(0, PLANES // CHUNK, some_planes, 0)

    def fold(index):
        return jnp.where(index <= NG // 2, index, index - NG).astype(f32)

    def prepare_scale():
        step = 2.0 * math.pi / CELL_BOHR
        second = fold(lax.broadcasted_iota(jnp.int32, (NG, 128), 0))
        third = fold(lax.broadcasted_iota(jnp.int32, (NG, 128), 1))
        flat = second * second + third * third

        def column(v, carry):
            first = (me * COLS + v).astype(f32)
            square = step**2 * (flat + first * first)
            safe = jnp.where(square > 0, square, 1.0)
            scale[v] = jnp.where(square > 0, 4.0 * math.pi / safe, 0.0)
            return carry

        lax.fori_loop(0, COLS, column, 0)

    @pl.when(core + odd > 0)
    def _():
        pl.semaphore_wait(go_sem, 2)

    for o in range(2):
        for part in range(2):
            for kind in range(2):
                in_copy(kind, o, part).start()
    prepare_scale()

    for kind in range(2):
        for part in range(2):
            in_copy(kind, 0, part).wait_recv()
    unpack(own_in, own, 0)
    unpack(vis_in, vis, 0)
    forward(0)
    start_group(0, 0)

    for kind in range(2):
        for o, part in ((0, 0), (0, 1), (1, 0)):
            in_copy(kind, o, part).wait_send()

    @pl.when(odd == 0)
    def _():
        for other in beside[:2]:
            pl.semaphore_signal(go_sem, 1, device_id=(other, me), device_id_type=MESH)

    @pl.when((odd == 1) & (core == 0))
    def _():
        for other in beside[2:]:
            pl.semaphore_signal(go_sem, 1, device_id=(other, me), device_id_type=MESH)

    wait_group(0, 0)
    middle(0)
    start_group(1, 0)

    for kind in range(2):
        in_copy(kind, 1, 1).wait_send()

    for part in range(2):
        in_copy(1, 1, part).wait_recv()
    unpack(vis_in, vis, 1)
    forward(1)
    start_group(0, 1)
    for part in range(2):
        in_copy(0, 1, part).wait_recv()
    unpack(own_in, own, 1)
    forward(2)
    start_group(0, 2)
    forward(3)
    start_group(0, 3)
    wait_group(1, 0)
    inverse(0)
    for pair in range(1, 4):
        wait_group(0, pair)
        middle(pair)
        start_group(1, pair)
    wait_group(1, 1)
    inverse(1)
    pack(near, 0, 0)
    out_copy(0, 0).start()
    wait_group(1, 2)
    inverse(2)
    pack(far, 1, 0)
    out_copy(1, 0).start()
    wait_group(1, 3)
    inverse(3)
    pack(near, 0, 1)
    out_copy(0, 1).start()
    pack(far, 1, 1)
    out_copy(1, 1).start()

    for stage in range(2):
        for pair in range(4):
            wait_group_sent(stage, pair)
    for o in range(2):
        for kind in range(2):
            out_copy(kind, o).wait_recv()
    for o in range(2):
        for kind in range(2):
            out_copy(kind, o).wait_send()


def body(orbitals):
    bands = lax.axis_size("band")
    steps = bands // 8
    whole = pl.BlockSpec(memory_space=pltpu.VMEM)
    lines = NG * PLANES
    dma = pltpu.SemaphoreType.DMA
    by_plane = orbitals.transpose(1, 0, 2)
    sums = jax.ShapeDtypeStruct(by_plane.shape, f32)
    near, far = pl.pallas_call(
        functools.partial(kernel_body, steps, bands),
        out_shape=(sums, sums),
        in_specs=[pl.BlockSpec(memory_space=pl.ANY)] + [whole] * 6,
        out_specs=(pl.BlockSpec(memory_space=pl.ANY), pl.BlockSpec(memory_space=pl.ANY)),
        scratch_shapes=[
            pltpu.VMEM((2, PLANES, NG * NG), f32),
            pltpu.VMEM((2, PLANES, NG * NG), f32),
            pltpu.VMEM((2, lines, 128), f32),
            pltpu.VMEM((2, lines, 128), f32),
            pltpu.VMEM((2, lines, 128), f32),
            pltpu.VMEM((2, lines, 128), f32),
            pltpu.VMEM((COLS, NG, 128), f32),
            pltpu.VMEM((4, 2, GROUP * SPAN, 128), f32),
            pltpu.VMEM((4, 2, GROUP * SPAN, 128), f32),
            pltpu.VMEM((4, 2, GROUP * SPAN, 128), f32),
            pltpu.VMEM((4, 2, GROUP * SPAN, 128), f32),
            pltpu.VMEM((2, 2, PLANES, NG * NG), f32),
            dma((2, 2, 2)),
            dma((2, 2, 2)),
            dma((4, GROUP)),
            dma((4, GROUP)),
            dma((4, GROUP)),
            dma((4, GROUP)),
            dma((2, 2)),
            dma((2, 2)),
            dma((2, 4)),
            pltpu.SemaphoreType.REGULAR,
        ],
        compiler_params=pltpu.CompilerParams(
            collective_id=0, has_side_effects=True, vmem_limit_bytes=56 << 20
        ),
    )(by_plane, *(jnp.asarray(t) for t in tables()))
    return (near + far).transpose(1, 0, 2)


def solution(mesh):
    return jax.shard_map(
        body,
        mesh=mesh,
        in_specs=(P("band", "fft", None),),
        out_specs=P("band", "fft", None),
        check_vma=False,
    )
```

```python
import functools
import math

import jax
import jax.numpy as jnp
import ml_dtypes
import numpy as np
from jax import lax
from jax.experimental import pallas as pl
from jax.experimental.pallas import tpu as pltpu
from jax.sharding import PartitionSpec as P

NG = 120
PLANES = 15
HALF = 64
GROUP = 8
COLS = HALF // GROUP
SPAN = PLANES * COLS
CHUNK = 5
FRACTION = 0.25
CELL_BOHR = 37.25
MESH = pl.DeviceIdType.MESH
f32, bf16 = jnp.float32, jnp.bfloat16


def split_const(table):
    high = table.astype(np.float32).astype(ml_dtypes.bfloat16)
    low = (table - high.astype(np.float64)).astype(np.float32).astype(ml_dtypes.bfloat16)
    return high, low


def on_left(table):
    high, low = split_const(table)
    return np.concatenate([high, high, low], axis=1)


def on_right(table):
    high, low = split_const(table)
    return np.concatenate([high, high, low], axis=0)


def tables():
    n = np.arange(NG)
    phase = (n[:, None] * n[None, :] % NG) * (2.0 * math.pi / NG)
    cos, sin = np.cos(phase), np.sin(phase)
    half = NG // 2 + 1
    first = np.zeros((2 * HALF, 128))
    first[:half, :NG] = cos[:half]
    first[HALF : HALF + half, :NG] = -sin[:half]
    wide_cos, wide_sin = np.zeros((128, 128)), np.zeros((128, 128))
    wide_cos[:NG, :NG], wide_sin[:NG, :NG] = cos, sin
    second = np.block([[wide_cos, -wide_sin], [wide_sin, wide_cos]])
    third = np.block([[cos, sin], [-sin, cos]])
    weight = np.full(half, 2.0)
    weight[[0, -1]] = 1.0
    weight *= -FRACTION / NG**3
    last = np.zeros((NG, 2 * HALF))
    last[:, :half] = cos[:, :half] * weight
    last[:, HALF : HALF + half] = -sin[:, :half] * weight
    return (
        on_left(first),
        on_right(second),
        on_left(third),
        on_left(third.T),
        on_right(second.T),
        on_left(last),
    )


def split(value):
    high = value.astype(bf16)
    return high, (value - high.astype(f32)).astype(bf16)


def left_dot(table, value):
    high, low = split(value)
    return jnp.dot(table, jnp.concatenate([high, low, high], axis=0), preferred_element_type=f32)


def right_dot(value, table):
    high, low = split(value)
    return jnp.dot(jnp.concatenate([high, low, high], axis=1), table, preferred_element_type=f32)


def kernel_body(
    steps,
    bands,
    x_ref,
    first_ref,
    second_ref,
    third_ref,
    third_back_ref,
    second_back_ref,
    last_ref,
    near_ref,
    far_ref,
    own_in,
    vis_in,
    own,
    vis,
    near,
    far,
    scale,
    send_a,
    got_a,
    send_b,
    got_b,
    packed,
    in_send,
    in_recv,
    a_send,
    a_recv,
    b_send,
    b_recv,
    out_send,
    out_recv,
    keep_sem,
    go_sem,
):
    band = lax.axis_index("band")
    me = lax.axis_index("fft")
    core = lax.rem(band, 2)
    up = lax.rem(band + steps, bands)
    down = lax.rem(band + bands - steps, bands)
    mate = band + 1 - 2 * core
    chip = bands // 16
    odd = lax.rem(lax.div(band, chip), 2)
    beside = [
        lax.rem(first + step + bands, bands) for first in (band, mate) for step in (chip, -chip)
    ]

    barrier = pltpu.get_barrier_semaphore()
    for other in (up, down, *beside):
        pl.semaphore_signal(barrier, 1, device_id=(other, me), device_id_type=MESH)
    for r in range(1, GROUP):
        pl.semaphore_signal(
            barrier, 1, device_id=(band, lax.rem(me + r, GROUP)), device_id_type=MESH
        )
    pl.semaphore_wait(barrier, GROUP + 5)

    def in_copy(kind, o, part):
        place = pl.ds(*((0, 11264), (11264, 3136))[part])
        return pltpu.make_async_remote_copy(
            x_ref.at[:, o, place],
            (own_in, vis_in)[kind].at[o, :, place],
            in_send.at[kind, o, part],
            in_recv.at[kind, o, part],
            device_id=((down, up)[kind], me),
            device_id_type=MESH,
        )

    def out_copy(kind, o, part):
        place = pl.ds(*((0, 7680), (7680, 6720))[part])
        return pltpu.make_async_remote_copy(
            packed.at[kind, o, :, place],
            (near_ref, far_ref)[kind].at[:, o, place],
            out_send.at[kind, o, part],
            out_recv.at[kind, o, part],
            device_id=((up, down)[kind], me),
            device_id_type=MESH,
        )

    def group_copy(sent, got, send_sem, recv_sem, pair, r):
        other = lax.rem(me + r, GROUP)
        return pltpu.make_async_remote_copy(
            sent.at[pair, :, pl.ds(pl.multiple_of(other * SPAN, 8), SPAN), :],
            got.at[pair, :, pl.ds(pl.multiple_of(me * SPAN, 8), SPAN), :],
            send_sem.at[pair, r],
            recv_sem.at[pair, r],
            device_id=(band, other),
            device_id_type=MESH,
        )

    def keep_copy(sent, got, stage, pair):
        place = pl.ds(pl.multiple_of(me * SPAN, 8), SPAN)
        return pltpu.make_async_copy(
            sent.at[pair, :, place, :], got.at[pair, :, place, :], keep_sem.at[stage, pair]
        )

    forth = (send_a, got_a, a_send, a_recv)
    return_trip = (send_b, got_b, b_send, b_recv)

    def start_group(stage, pair):
        arrays = (forth, return_trip)[stage]
        for r in range(1, GROUP):
            group_copy(*arrays, pair, r).start()
        keep_copy(arrays[0], arrays[1], stage, pair).start()

    def wait_group(stage, pair):
        arrays = (forth, return_trip)[stage]
        for r in range(1, GROUP):
            group_copy(*arrays, pair, r).wait_recv()
        keep_copy(arrays[0], arrays[1], stage, pair).wait()

    def wait_group_sent(stage, pair):
        arrays = (forth, return_trip)[stage]
        for r in range(1, GROUP):
            group_copy(*arrays, pair, r).wait_send()

    lane = lax.broadcasted_iota(jnp.int32, (PLANES, 128), 1)

    def unpack(source, target, o):
        def line(group, r, tile_start):
            if r == 0:
                return source[o, :, pl.ds(tile_start, 128)]
            before = source[o, :, pl.ds(tile_start - 128, 128)]
            if r == 16:
                return pltpu.roll(before, 128, 1)
            here = source[o, :, pl.ds(tile_start, 128)]
            return pltpu.roll(jnp.where(lane >= 128 - 8 * r, before, here), 8 * r, 1)

        def one_group(group, carry):
            for r in range(16):
                start = pl.multiple_of((group * 15 + r) * 128, 128)
                if r < 15:
                    value = line(group, r, start)
                else:
                    before = source[o, :, pl.ds(pl.multiple_of(start - 128, 128), 128)]
                    value = pltpu.roll(before, 120, 1)
                target[o, pl.ds(group * 16 + r, PLANES, stride=NG), :] = value
            return carry

        lax.fori_loop(0, 7, one_group, 0)
        for r in range(8):
            y = 112 + r
            if r < 7:
                value = line(7, r, (7 * 15 + r) * 128)
            else:
                value = jnp.concatenate(
                    [source[o, :, y * NG : (y + 1) * NG], jnp.zeros((PLANES, 8), f32)], axis=1
                )
            target[o, pl.ds(y, PLANES, stride=NG), :] = value

    def pack(source, kind, o, part):
        def tile(y, s, following):
            value = source[o, pl.ds(y, PLANES, stride=NG), :]
            if s:
                value = pltpu.roll(value, 128 - 8 * s, 1)
            if following is None:
                return value
            after = source[o, pl.ds(following, PLANES, stride=NG), :]
            return jnp.where(lane < NG - 8 * s, value, pltpu.roll(after, NG - 8 * s, 1))

        def one_group(group, carry):
            for s in range(15):
                y = group * 16 + s
                place = pl.ds(pl.multiple_of((group * 15 + s) * 128, 128), 128)
                packed[kind, o, :, place] = tile(y, s, y + 1)
            return carry

        lax.fori_loop(4 * part, (4, 7)[part], one_group, 0)
        for s in range(8 * part):
            y = 112 + s
            start = (105 + s) * 128
            if s < 7:
                packed[kind, o, :, start : start + 128] = tile(y, s, y + 1)
            else:
                packed[kind, o, :, start:] = tile(y, s, None)[:, : NG * NG - start]

    def plane(ref, o, p):
        return ref[o, pl.ds(pl.multiple_of(p * NG, 8), NG), :]

    def forward(pair):
        i, j = pair // 2, pair % 2

        def some_planes(step, carry):
            products = []
            for q in range(CHUNK):
                p = step * CHUNK + q
                product = plane(own, i, p) * plane(vis, j, p)
                products.append(jnp.concatenate([product, jnp.zeros((8, 128), f32)], axis=0))
            lines = left_dot(first_ref[...], jnp.concatenate(products, axis=1))
            lines = jnp.concatenate(
                [
                    jnp.concatenate(
                        [
                            lines[:HALF, q * 128 : (q + 1) * 128],
                            lines[HALF:, q * 128 : (q + 1) * 128],
                        ],
                        axis=1,
                    )
                    for q in range(CHUNK)
                ],
                axis=0,
            )
            spectrum = right_dot(lines, second_ref[...])
            for q in range(CHUNK):
                p = step * CHUNK + q
                for d in range(GROUP):
                    place = pl.ds(pl.multiple_of(d * SPAN + p * COLS, 8), COLS)
                    rows = slice(q * HALF + d * COLS, q * HALF + (d + 1) * COLS)
                    send_a[pair, 0, place, :] = spectrum[rows, :128]
                    send_a[pair, 1, place, :] = spectrum[rows, 128:]
            return carry

        lax.fori_loop(0, PLANES // CHUNK, some_planes, 0)

    def middle(pair):
        def two_columns(step, carry):
            columns = [step * 2, step * 2 + 1]
            data = jnp.concatenate(
                [
                    jnp.concatenate(
                        [
                            got_a[pair, 0, pl.ds(v, NG, stride=COLS), :],
                            got_a[pair, 1, pl.ds(v, NG, stride=COLS), :],
                        ],
                        axis=0,
                    )
                    for v in columns
                ],
                axis=1,
            )
            data = left_dot(third_ref[...], data)
            factor = jnp.concatenate([scale[v] for v in columns], axis=1)
            data = left_dot(
                third_back_ref[...], data * jnp.concatenate([factor, factor], axis=0)
            )
            for n, v in enumerate(columns):
                send_b[pair, 0, pl.ds(v, NG, stride=COLS), :] = data[
                    :NG, n * 128 : (n + 1) * 128
                ]
                send_b[pair, 1, pl.ds(v, NG, stride=COLS), :] = data[
                    NG:, n * 128 : (n + 1) * 128
                ]
            return carry

        lax.fori_loop(0, COLS // 2, two_columns, 0)

    def inverse(pair):
        i, j = pair // 2, pair % 2

        def some_planes(step, carry):
            spectra = []
            for q in range(CHUNK):
                p = step * CHUNK + q
                places = [pl.ds(pl.multiple_of(d * SPAN + p * COLS, 8), COLS) for d in range(GROUP)]
                spectra.append(
                    jnp.concatenate(
                        [
                            jnp.concatenate([got_b[pair, c, place, :] for place in places], axis=0)
                            for c in range(2)
                        ],
                        axis=1,
                    )
                )
            lines = right_dot(jnp.concatenate(spectra, axis=0), second_back_ref[...])
            lines = jnp.concatenate(
                [
                    jnp.concatenate(
                        [
                            lines[q * HALF : (q + 1) * HALF, :128],
                            lines[q * HALF : (q + 1) * HALF, 128:],
                        ],
                        axis=0,
                    )
                    for q in range(CHUNK)
                ],
                axis=1,
            )
            field = left_dot(last_ref[...], lines)
            for q in range(CHUNK):
                p = step * CHUNK + q
                value = field[:, q * 128 : (q + 1) * 128]
                to_near, to_far = plane(vis, j, p) * value, plane(own, i, p) * value
                if j:
                    to_near += plane(near, i, p)
                if i:
                    to_far += plane(far, j, p)
                near[i, pl.ds(pl.multiple_of(p * NG, 8), NG), :] = to_near
                far[j, pl.ds(pl.multiple_of(p * NG, 8), NG), :] = to_far
            return carry

        lax.fori_loop(0, PLANES // CHUNK, some_planes, 0)

    def fold(index):
        return jnp.where(index <= NG // 2, index, index - NG).astype(f32)

    def prepare_scale():
        step = 2.0 * math.pi / CELL_BOHR
        second = fold(lax.broadcasted_iota(jnp.int32, (NG, 128), 0))
        third = fold(lax.broadcasted_iota(jnp.int32, (NG, 128), 1))
        flat = second * second + third * third

        def column(v, carry):
            first = (me * COLS + v).astype(f32)
            square = step**2 * (flat + first * first)
            safe = jnp.where(square > 0, square, 1.0)
            scale[v] = jnp.where(square > 0, 4.0 * math.pi / safe, 0.0)
            return carry

        lax.fori_loop(0, COLS, column, 0)

    @pl.when(core + odd > 0)
    def _():
        pl.semaphore_wait(go_sem, 2)

    for o in range(2):
        for part in range(2):
            for kind in range(2):
                in_copy(kind, o, part).start()
    prepare_scale()

    for kind in range(2):
        for part in range(2):
            in_copy(kind, 0, part).wait_recv()
    unpack(own_in, own, 0)
    unpack(vis_in, vis, 0)
    forward(0)
    start_group(0, 0)

    for kind in range(2):
        for o, part in ((0, 0), (0, 1), (1, 0)):
            in_copy(kind, o, part).wait_send()

    @pl.when(odd == 0)
    def _():
        for other in beside[:2]:
            pl.semaphore_signal(go_sem, 1, device_id=(other, me), device_id_type=MESH)

    @pl.when((odd == 1) & (core == 0))
    def _():
        for other in beside[2:]:
            pl.semaphore_signal(go_sem, 1, device_id=(other, me), device_id_type=MESH)

    wait_group(0, 0)
    middle(0)
    start_group(1, 0)

    for kind in range(2):
        in_copy(kind, 1, 1).wait_send()

    for part in range(2):
        in_copy(1, 1, part).wait_recv()
    unpack(vis_in, vis, 1)
    forward(1)
    start_group(0, 1)
    for part in range(2):
        in_copy(0, 1, part).wait_recv()
    unpack(own_in, own, 1)
    forward(2)
    start_group(0, 2)
    forward(3)
    start_group(0, 3)
    wait_group(1, 0)
    inverse(0)
    for pair in range(1, 4):
        wait_group(0, pair)
        middle(pair)
        start_group(1, pair)
    wait_group(1, 1)
    inverse(1)
    for part in range(2):
        pack(near, 0, 0, part)
        out_copy(0, 0, part).start()
    wait_group(1, 2)
    inverse(2)
    for part in range(2):
        pack(far, 1, 0, part)
        out_copy(1, 0, part).start()
    wait_group(1, 3)
    inverse(3)
    for part in range(2):
        pack(near, 0, 1, part)
        out_copy(0, 1, part).start()
        pack(far, 1, 1, part)
        out_copy(1, 1, part).start()

    for stage in range(2):
        for pair in range(4):
            wait_group_sent(stage, pair)
    for o in range(2):
        for kind in range(2):
            for part in range(2):
                out_copy(kind, o, part).wait_recv()
    for o in range(2):
        for kind in range(2):
            for part in range(2):
                out_copy(kind, o, part).wait_send()


def body(orbitals):
    bands = lax.axis_size("band")
    steps = bands // 8
    whole = pl.BlockSpec(memory_space=pltpu.VMEM)
    lines = NG * PLANES
    dma = pltpu.SemaphoreType.DMA
    by_plane = orbitals.transpose(1, 0, 2)
    sums = jax.ShapeDtypeStruct(by_plane.shape, f32)
    near, far = pl.pallas_call(
        functools.partial(kernel_body, steps, bands),
        out_shape=(sums, sums),
        in_specs=[pl.BlockSpec(memory_space=pl.ANY)] + [whole] * 6,
        out_specs=(pl.BlockSpec(memory_space=pl.ANY), pl.BlockSpec(memory_space=pl.ANY)),
        scratch_shapes=[
            pltpu.VMEM((2, PLANES, NG * NG), f32),
            pltpu.VMEM((2, PLANES, NG * NG), f32),
            pltpu.VMEM((2, lines, 128), f32),
            pltpu.VMEM((2, lines, 128), f32),
            pltpu.VMEM((2, lines, 128), f32),
            pltpu.VMEM((2, lines, 128), f32),
            pltpu.VMEM((COLS, NG, 128), f32),
            pltpu.VMEM((4, 2, GROUP * SPAN, 128), f32),
            pltpu.VMEM((4, 2, GROUP * SPAN, 128), f32),
            pltpu.VMEM((4, 2, GROUP * SPAN, 128), f32),
            pltpu.VMEM((4, 2, GROUP * SPAN, 128), f32),
            pltpu.VMEM((2, 2, PLANES, NG * NG), f32),
            dma((2, 2, 2)),
            dma((2, 2, 2)),
            dma((4, GROUP)),
            dma((4, GROUP)),
            dma((4, GROUP)),
            dma((4, GROUP)),
            dma((2, 2, 2)),
            dma((2, 2, 2)),
            dma((2, 4)),
            pltpu.SemaphoreType.REGULAR,
        ],
        compiler_params=pltpu.CompilerParams(
            collective_id=0, has_side_effects=True, vmem_limit_bytes=56 << 20
        ),
    )(by_plane, *(jnp.asarray(t) for t in tables()))
    return (near + far).transpose(1, 0, 2)


def solution(mesh):
    return jax.shard_map(
        body,
        mesh=mesh,
        in_specs=(P("band", "fft", None),),
        out_specs=P("band", "fft", None),
        check_vma=False,
    )
```
